32 devices in a mesh: bins: 4 (over z), chan: 4 (over y, x), seqs: 2 (over core).
Axes of the slice: x: 2, y: 2, z: 4, core: 2. Of those that a mesh axis runs over, the one named last changes fastest.
Arguments:
- inputs: bfloat16 [8, 1024, 768], P('seqs', 'bins'), may hold values from -30 to 30
- valid_bins: int32 [8, 1024], P('seqs', 'bins'), may hold values from 0 to 1, as said below
- cotangent: bfloat16 [8, 1024, 768], P('seqs', 'bins'), may hold values from -6 to 6
- conv1_weight: float32 [2304, 384], P(None, 'chan'), may hold values from -0.125 to 0.125
- conv1_momentum: float32 [2304, 384], P(None, 'chan'), may hold values from -1280 to 1280
- conv2_weight: float32 [384, 768], P('chan'), may hold values from -0.625 to 0.625
- conv2_momentum: float32 [384, 768], P('chan'), may hold values from -320 to 320
- norm1_params: float32 [2, 768], replicated, may hold values from -1 to 2, as said below
- norm1_momentum: float32 [2, 768], replicated, may hold values from -112 to 112
- norm2_params: float32 [2, 384], P(None, 'chan'), may hold values from -1 to 2, as said below
- norm2_momentum: float32 [2, 384], P(None, 'chan'), may hold values from -128 to 128
Outputs:
- output: bfloat16 [8, 1024, 768], P('seqs', 'bins')
- input_grad: float32 [8, 1024, 768], P('seqs', 'bins')
- conv1_moment: float32 [2304, 384], P(None, 'chan')
- conv1_new: float32 [2304, 384], P(None, 'chan')
- conv1_low: bfloat16 [2304, 384], P(None, 'chan')
- conv2_moment: float32 [384, 768], P('chan')
- conv2_new: float32 [384, 768], P('chan')
- conv2_low: bfloat16 [384, 768], P('chan')
- norm1_moment: float32 [2, 768], replicated
- norm1_new: float32 [2, 768], replicated
- norm2_moment: float32 [2, 384], P(None, 'chan')
- norm2_new: float32 [2, 384], P(None, 'chan')
The draws below stay inside these ranges and needn't reach their ends.
Inputs may be any that keep to these rules, and one draw needn't show every extreme that they name: `valid_bins`: 1 marks a valid bin; the first bin of every sequence is valid. `norm1_params`: gains lie in 0.6 to 1.6. `norm2_params`: gains lie in 0.6 to 1.6.
All inputs are finite; a program needn't handle non-finite values.
Results may differ from the reference program's by a relative error of at most 0.0078.
Values may be sent and summed in bfloat16 or wider, within the bound.
No kernel may reach another device: no remote copies, remote signals or barrier semaphores. Data moves between devices by JAX's collectives and lax.ppermute only.
A program may use at most 64 MiB of HBM per device.

```python
import math
import jax
import jax.numpy as jnp
from jax import lax

C = 768
HID = 384
KERNEL_TAPS = 3
DILATION_STEP = 28
NS_ITERS = 5
SEQUENCE_BINS = 1024
SEQS = 8


def valid_pattern(key):
    ticks = jax.random.randint(key, (SEQS, SEQUENCE_BINS), 0, 1000)
    place = jnp.arange(SEQUENCE_BINS, dtype=jnp.int32)[None, :]
    limit = 300 + 600 * place // SEQUENCE_BINS
    return jnp.logical_or(ticks < limit, place == 0).astype(jnp.int32)


def draw_valid_bins(key, part):
    return valid_pattern(key)


def draw_inputs(key, part):
    pattern = valid_pattern(key)
    key = jax.random.fold_in(key, 11)
    place = jnp.arange(SEQUENCE_BINS, dtype=jnp.float32) / SEQUENCE_BINS
    noise = jax.random.truncated_normal(key, -6.0, 6.0, (SEQS, SEQUENCE_BINS, C), jnp.float32)
    growth = 1.0 + 2.0 * place
    offset = 1.5 * (1.0 - pattern.astype(jnp.float32))[:, :, None]
    return (growth[None, :, None] * (noise + offset)).astype(jnp.bfloat16)


def norm_pair(key, count):
    gain_key, bias_key = jax.random.split(key)
    gains = jax.random.uniform(gain_key, (count,), jnp.float32, 0.6, 1.6)
    biases = 0.3 * jax.random.truncated_normal(bias_key, -3.0, 3.0, (count,), jnp.float32)
    return jnp.stack([gains, biases])


def draw_norm1_params(key, part):
    key = jax.random.fold_in(key, 21)
    return norm_pair(key, C)


def draw_norm2_params(key, part):
    key = jax.random.fold_in(key, 22)
    return norm_pair(key, HID)


def level_of(key, shape, cuts, low, top_value):
    factor_of = 1.0
    for position, blocks in cuts:
        steps = jax.random.uniform(jax.random.fold_in(jax.random.fold_in(key, 6), position), (blocks,), jnp.float32, low / len(cuts), top_value / len(cuts))
        factor_of = factor_of * jnp.repeat(jnp.exp(steps), shape[position] // blocks).reshape((-1,) + (1,) * (len(shape) - 1 - position))
    return factor_of


def centred(key, dims, scale, most, cuts=(), kind=jnp.bfloat16):
    values = scale * jax.random.normal(key, dims, jnp.float32)
    if cuts:
        values = values * level_of(key, dims, cuts, -0.22, 0.18)
    return jnp.clip(values, -most, most).astype(kind)


def setup_inputs(seed: int = 0) -> dict:
    key_of = jax.random.split(jax.random.key(seed), 12)
    return {
        "inputs": draw_inputs(jax.random.fold_in(key_of[11], 71), 0),
        "valid_bins": draw_valid_bins(jax.random.fold_in(key_of[11], 71), 0),
        "cotangent": centred(key_of[2], (SEQS, SEQUENCE_BINS, C), 1.0, 6.0, ((0, 2), (1, 4))),
        "conv1_weight": centred(key_of[3], (KERNEL_TAPS * C, HID), (KERNEL_TAPS * C) ** -0.5, 0.125, ((1, 4),), jnp.float32),
        "conv1_momentum": centred(key_of[4], (KERNEL_TAPS * C, HID), (2.2 * (SEQS * SEQUENCE_BINS) ** 0.5), 1280.0, ((1, 4),), jnp.float32),
        "conv2_weight": centred(key_of[5], (HID, C), (HID // 4) ** -0.5, 0.625, ((0, 4),), jnp.float32),
        "conv2_momentum": centred(key_of[6], (HID, C), (0.65 * (SEQS * SEQUENCE_BINS) ** 0.5), 320.0, ((0, 4),), jnp.float32),
        "norm1_params": draw_norm1_params(jax.random.fold_in(key_of[11], 71), 0),
        "norm1_momentum": centred(key_of[8], (2, C), (0.2 * (SEQS * SEQUENCE_BINS) ** 0.5), 112.0, (), jnp.float32),
        "norm2_params": draw_norm2_params(jax.random.fold_in(key_of[11], 71), 0),
        "norm2_momentum": centred(key_of[10], (2, HID), (0.25 * (SEQS * SEQUENCE_BINS) ** 0.5), 128.0, ((1, 4),), jnp.float32),
    }


@jax.custom_vjp
def low(v):
    return lax.optimization_barrier(v.astype(jnp.bfloat16)).astype(jnp.float32)

@jax.custom_vjp
def low_back(v):
    return v

def low_keep(v):
    return (low(v), None)

def low_pass(kept, grad):
    return (grad,)

def back_keep(v):
    return (v, None)

def back_low(kept, grad):
    return (low(grad),)
low.defvjp(low_keep, low_pass)
low_back.defvjp(back_keep, back_low)
NORM_EPSILON = 0.001
GUARD_EPSILON = 1e-07
MOMENT_CONV = 0.95
RATE_CONV = 0.3
MOMENT_NORM = 0.9
RATE_NORM = 0.001
NEWTON_A = 3.4445
NEWTON_B = -4.775
NEWTON_C = 2.0315

def smooth(value):
    return value * jax.nn.sigmoid(1.702 * value)

def normalize(value, params, valid_col, counted):
    total = lax.optimization_barrier(jnp.sum(valid_col * value, axis=(0, 1)))
    squares = lax.optimization_barrier(jnp.sum(valid_col * value * value, axis=(0, 1)))
    mean_value = total / counted
    spread = squares / counted - mean_value * mean_value
    return params[0] * ((value - mean_value) * lax.rsqrt(spread + NORM_EPSILON)) + params[1]

def dilated(activated_input, weight):
    padded_input = jnp.pad(activated_input, ((0, 0), (DILATION_STEP, DILATION_STEP), (0, 0)))
    column_stack = jnp.concatenate([padded_input[:, kernel_tap_index * DILATION_STEP:kernel_tap_index * DILATION_STEP + SEQUENCE_BINS, :] for kernel_tap_index in range(KERNEL_TAPS)], axis=2)
    return jnp.einsum('slk,kh->slh', column_stack, weight, precision=lax.Precision.HIGHEST)

def orthogonal(matrix):
    gram = jnp.dot(matrix.T, matrix, precision=lax.Precision.HIGHEST)
    scale = jnp.sqrt(jnp.trace(gram)) + GUARD_EPSILON
    matrix = matrix / scale
    square_form = gram / (scale * scale)
    for sweep_no in range(NS_ITERS):
        polynomial = NEWTON_B * square_form + NEWTON_C * jnp.dot(square_form, square_form, precision=lax.Precision.HIGHEST)
        matrix = NEWTON_A * matrix + jnp.dot(matrix, polynomial, precision=lax.Precision.HIGHEST)
        if sweep_no < NS_ITERS - 1:
            square_form = jnp.dot(matrix.T, matrix, precision=lax.Precision.HIGHEST)
    return matrix

def reference(inputs, valid_bins, cotangent, conv1_weight, conv1_momentum, conv2_weight, conv2_momentum, norm1_params, norm1_momentum, norm2_params, norm2_momentum):
    valid_col = valid_bins.astype(jnp.float32)[:, :, None]
    counted = jnp.sum(valid_col)

    def forward(feature, first_weight, second_weight, first_params, second_params):
        activated_input = low(smooth(normalize(feature, first_params, valid_col, counted)))
        hidden = low_back(dilated(activated_input, low(first_weight)))
        mixed = low(smooth(normalize(hidden, second_params, valid_col, counted)))
        branch = jnp.einsum('slh,hc->slc', mixed, low(second_weight), precision=lax.Precision.HIGHEST)
        return feature + branch
    result, pullback = jax.vjp(forward, inputs.astype(jnp.float32), conv1_weight, conv2_weight, norm1_params, norm2_params)
    input_grad, grad_first, grad_second, grad_norm_one, grad_norm_two = pullback(cotangent.astype(jnp.float32))
    norm1_moment = MOMENT_NORM * norm1_momentum + grad_norm_one
    norm1_new = norm1_params - RATE_NORM * norm1_moment
    norm2_moment = MOMENT_NORM * norm2_momentum + grad_norm_two
    norm2_new = norm2_params - RATE_NORM * norm2_moment
    conv1_moment = MOMENT_CONV * conv1_momentum + grad_first
    conv2_moment = MOMENT_CONV * conv2_momentum + grad_second
    rate_first = RATE_CONV * math.sqrt(max(1.0, KERNEL_TAPS * C / HID))
    rate_second = RATE_CONV * math.sqrt(max(1.0, C / HID))
    conv1_new = conv1_weight - rate_first * orthogonal(conv1_moment)
    conv2_new = conv2_weight - rate_second * orthogonal(conv2_moment.T).T
    return (result.astype(jnp.bfloat16), input_grad, conv1_moment, conv1_new, conv1_new.astype(jnp.bfloat16), conv2_moment, conv2_new, conv2_new.astype(jnp.bfloat16), norm1_moment, norm1_new, norm2_moment, norm2_new)
```

```python
import functools
import math

import jax
import jax.numpy as jnp
from jax import lax
from jax.experimental import pallas as pl
from jax.experimental.pallas import tpu as pltpu
from jax.sharding import PartitionSpec as P

DILATION_STEP = 28
NS_ITERS = 5

NORM_EPSILON = 0.001
GUARD_EPSILON = 1e-07
MOMENT_CONV = 0.95
RATE_CONV = 0.3
MOMENT_NORM = 0.9
RATE_NORM = 0.001
NEWTON_A = 3.4445
NEWTON_B = -4.775
NEWTON_C = 2.0315
HALO = 32
LANES = 128
F32 = jnp.float32
BF16 = jnp.bfloat16


def flipped(value, axis, mask):
    count = lax.axis_size(axis)
    return lax.ppermute(value, axis, [(i, i ^ mask) for i in range(count)])


def short(axis):
    return lax.axis_size(axis) == 4


def partners(value, axis):
    rest = [flipped(value, axis, mask) for mask in range(lax.axis_size(axis) - 1, 0, -1)]
    return [value] + rest[::-1]


def summed(parts):
    parts = list(parts)
    while len(parts) > 1:
        parts = [parts[i] + parts[i + 1] for i in range(0, len(parts), 2)]
    return parts[0]


def terms(value):
    return partners(value, "bins") if short("bins") else [lax.psum(value, "bins")]


def doubled(value, mask=1, ahead=()):
    if not short("bins"):
        return lax.psum(value, "bins"), ahead
    while mask < lax.axis_size("bins"):
        if 2 * mask == lax.axis_size("bins"):
            value, ahead = tied(value, ahead)
        value = value + flipped(value, "bins", mask)
        mask *= 2
    return value, ahead


def tied(*values):
    return lax.optimization_barrier(values)


def exchanged(first, second):
    count, cores = lax.axis_size("bins"), lax.axis_size("seqs")

    def to(start):
        pairs = []
        for z in range(count):
            other = z + 1 if (z - start) % 2 == 0 else z - 1
            for core in range(cores):
                inside = 0 <= other < count
                target = other * cores + core if inside else z * cores + (core ^ 1)
                pairs.append((z * cores + core, target))
        return pairs

    return [lax.ppermute(value, ("bins", "seqs"), to(start)) for start, value in enumerate((first, second))]


def even(axis):
    return lax.rem(lax.axis_index(axis), 2) == 0


def dot(left, right):
    return lax.dot_general(left, right, (((1,), (0,)), ((), ())), preferred_element_type=F32)


def dot_rows(left, right):
    return lax.dot_general(left, right, (((1,), (1,)), ((), ())), preferred_element_type=F32)


def dot_columns(left, right):
    return lax.dot_general(left, right, (((0,), (0,)), ((), ())), preferred_element_type=F32)


def sigmoid(value):
    return 0.5 + 0.5 * jnp.tanh(0.851 * value)


def mask_of(valid_ref, i):
    valid = valid_ref[i : i + 1, :].astype(F32)
    return jnp.broadcast_to(valid, (LANES, valid.shape[1])).T


def rows_of(*parts):
    width = parts[0].shape[1]
    return jnp.concatenate(list(parts) + [jnp.zeros((8 - len(parts), width), F32)], axis=0)


def put_edges(first_ref, second_ref, i, head, tail):
    to_next = even("bins")
    first_ref[i] = jnp.where(to_next, tail, head)
    second_ref[i] = jnp.where(to_next, head, tail)


def inner(count):
    place = lax.axis_index("bins")
    return (place > 0).astype(F32), (place < count - 1).astype(F32)


def edges_of(first_ref, second_ref, i):
    to_next = even("bins")
    first, second = first_ref[i].astype(F32), second_ref[i].astype(F32)
    return jnp.where(to_next, second, first), jnp.where(to_next, first, second)


def stats_kernel(x_any, valid_any, sums_ref, first_ref, second_ref, x_ref, valid_ref, arrived):
    seqs, bins, width = x_ref.shape
    copies = [pltpu.make_async_copy(valid_any, valid_ref, arrived.at[seqs])] + [
        pltpu.make_async_copy(x_any.at[i], x_ref.at[i], arrived.at[i]) for i in range(seqs)
    ]
    for copy in copies:
        copy.start()
    copies.pop(0).wait()
    first = second = count = 0.0
    for i in range(seqs):
        mask = mask_of(valid_ref, i)
        copies[i].wait()
        kept = x_ref[i].astype(F32) * jnp.concatenate([mask] * (width // LANES), axis=1)
        first += jnp.sum(kept, axis=0, keepdims=True)
        second += jnp.sum(kept * kept, axis=0, keepdims=True)
        count += jnp.sum(mask, axis=0, keepdims=True)
        put_edges(first_ref, second_ref, i, x_ref[i, :HALO, :], x_ref[i, bins - HALO :, :])
    sums_ref[...] = rows_of(first, second, jnp.concatenate([count] * (width // LANES), axis=1))


def prep_kernel(after_ref, *refs):
    out_ref, other_ref, first_ref, second_ref, *held = refs[4:12]
    arrived = refs[12]
    copies = [
        pltpu.make_async_copy(ref, buffer, arrived.at[i])
        for i, (ref, buffer) in enumerate(zip(refs[:4], held))
    ]
    for copy in copies:
        copy.start()
    weight_one, weight_two, momentum_one, momentum_two = held
    split, width = weight_one.shape[1], weight_two.shape[1]
    half = (split + width) // 2

    def put(ref, start, value):
        ref[:, start : start + value.shape[1]] = value.astype(BF16)

    def put_two(start, value):
        high, low = split2(value)
        put(out_ref, half + start, high)
        put(out_ref, 2 * half + start, low)

    def put_low(ref):
        put(ref, 0, weight_one[:, :half])

    def put_high(ref):
        put(ref, 0, weight_one[:, half:])
        put(ref, split - half, weight_two[...])

    for copy in copies[:2]:
        copy.wait()
    own = weight_one.shape[0]
    for k in range(split // width):
        first_ref[k * LANES : k * LANES + own, :] = weight_one[:, k * width : (k + 1) * width].astype(BF16)
        first_ref[k * LANES + own : (k + 1) * LANES, :] = jnp.zeros((LANES - own, width), BF16)
    second_ref[:own, :] = weight_two[...].astype(BF16)
    second_ref[own:, :] = jnp.zeros((LANES - own, width), BF16)
    for copy in copies[2:]:
        copy.wait()
    side = lax.axis_index("seqs")

    @pl.when(side == 0)
    def _():
        put_low(out_ref)
        put_high(other_ref)
        put_two(0, momentum_one[:, :half])

    @pl.when(side != 0)
    def _():
        put_high(out_ref)
        put_low(other_ref)
        put_two(0, momentum_one[:, half:])
        put_two(split - half, momentum_two[...])


def conv_kernel(parts, count, *refs):
    pieces = refs[:parts]
    (x_ref, first_ref, second_ref, params_ref, low_ref, valid_ref,
     act_ref, hidden_ref, sums_ref, stat_ref, wide_ref) = refs[parts:]
    seqs, bins, width = x_ref.shape
    taps = low_ref.shape[0] // LANES
    sums = summed([p[...] for p in pieces])
    counted = sums[2:3]
    mean = sums[0:1] / counted
    rstd = lax.rsqrt(sums[1:2] / counted - mean * mean + NORM_EPSILON)
    gain = params_ref[0:1, :] * rstd
    bias = params_ref[1:2, :] - mean * gain
    stat_ref[...] = rows_of(mean, rstd, counted, gain, bias)
    first, last = inner(count)

    def activated(cells):
        value = cells.astype(F32) * gain + bias
        return value * sigmoid(value)

    total = squares = 0.0
    for i in range(seqs):
        before, after = edges_of(first_ref, second_ref, i)
        act_ref[i, :HALO, :] = (activated(before) * first).astype(BF16)
        act_ref[i, HALO : HALO + bins, :] = activated(x_ref[i]).astype(BF16)
        act_ref[i, HALO + bins :, :] = (activated(after) * last).astype(BF16)
        wide_ref[...] = dot_rows(act_ref[i], low_ref[...])
        hidden = 0.0
        for k in range(taps):
            start = HALO + (k - taps // 2) * DILATION_STEP
            hidden += wide_ref[start : start + bins, k * LANES : (k + 1) * LANES]
        hidden_ref[i * bins : (i + 1) * bins, :] = hidden
        kept = mask_of(valid_ref, i) * hidden
        total += jnp.sum(kept, axis=0, keepdims=True)
        squares += jnp.sum(kept * hidden, axis=0, keepdims=True)
    sums_ref[...] = rows_of(total, squares)


def back_kernel(upstream_ref, low_ref, out_ref):
    out_ref[...] = dot_rows(upstream_ref[...], low_ref[...])


def mix_kernel(parts, *refs):
    pieces = refs[:parts]
    (stat_one_ref, params_ref, hidden_ref, back_ref,
     mixed_ref, grad_ref, sums_ref, stat_ref) = refs[parts:]
    sums = summed([p[...] for p in pieces])
    counted = stat_one_ref[2:3, :LANES]
    mean = sums[0:1] / counted
    rstd = lax.rsqrt(sums[1:2] / counted - mean * mean + NORM_EPSILON)
    stat_ref[...] = rows_of(mean, rstd, counted)
    norm = (hidden_ref[...] - mean) * rstd
    value = params_ref[0:1, :] * norm + params_ref[1:2, :]
    sigma = sigmoid(value)
    mixed = value * sigma
    mixed_ref[...] = mixed.astype(BF16)
    grad = back_ref[...] * (sigma + 1.702 * mixed * (1.0 - sigma))
    grad_ref[...] = grad
    sums_ref[...] = rows_of(
        jnp.sum(grad * norm, axis=0, keepdims=True), jnp.sum(grad, axis=0, keepdims=True)
    )


def grads_kernel(parts, *refs):
    pieces = refs[:parts]
    (stat_ref, params_ref, hidden_ref, grad_ref, valid_ref, mixed_ref, act_ref, upstream_ref,
     keep_ref, give_ref, grad_low_ref, first_ref, second_ref, shift_ref) = refs[parts:]
    seqs, padded, width = act_ref.shape
    bins = padded - 2 * HALO
    taps = shift_ref.shape[1] // LANES
    own = keep_ref.shape[0]
    sums = summed([p[...] for p in pieces])
    mean, rstd, counted = stat_ref[0:1, :], stat_ref[1:2, :], stat_ref[2:3, :]
    mask = jnp.concatenate([mask_of(valid_ref, i) for i in range(seqs)], axis=0)
    norm = (hidden_ref[...] - mean) * rstd
    grad = rstd * params_ref[0:1, :] * (
        grad_ref[...] - mask / counted * (sums[1:2] + norm * sums[0:1])
    )
    low = grad.astype(BF16)
    grad = low.astype(F32)
    grad_low_ref[...] = low
    for i in range(seqs):
        part = grad[i * bins : (i + 1) * bins, :]
        put_edges(
            first_ref, second_ref, i, part[:HALO].astype(BF16), part[bins - HALO :].astype(BF16)
        )
        for k in range(taps):
            start = HALO + (k - taps // 2) * DILATION_STEP
            lanes = slice(k * LANES, (k + 1) * LANES)
            base = i * padded
            shift_ref[base : base + start, lanes] = jnp.zeros((start, LANES), F32)
            shift_ref[base + start : base + start + bins, lanes] = part
            shift_ref[base + start + bins : base + padded, lanes] = jnp.zeros(
                (padded - start - bins, LANES), F32
            )
    act = act_ref[...].reshape(seqs * padded, width)
    first = dot_columns(shift_ref[...].astype(BF16), act)
    second = dot_columns(mixed_ref[...], upstream_ref[...])
    both = [first[k * LANES : k * LANES + own, :] for k in range(taps)] + [second[:own, :]]
    count = len(both) // 2

    def put(ref, blocks):
        for k, block in enumerate(blocks):
            ref[:, k * width : (k + 1) * width] = block.astype(ref.dtype)

    side = lax.axis_index("seqs")

    @pl.when(side == 0)
    def _():
        put(keep_ref, both[:count])
        put(give_ref, both[count:])

    @pl.when(side != 0)
    def _():
        put(keep_ref, both[count:])
        put(give_ref, both[:count])


def pair_kernel(keep_ref, give_ref, first_ref, second_ref, *outs):
    place = lax.axis_index("bins")
    own, size = outs[0].shape
    for mask, out in enumerate(outs):
        columns = pl.ds(pl.multiple_of((place ^ mask) * size, LANES), size)
        out[:own, :] = (keep_ref[:, columns] + give_ref[:, columns].astype(F32)).astype(BF16)
    for out, edge in ((outs[1], first_ref), (outs[3], second_ref)):
        rows = edge[...].reshape(-1, LANES)
        depth = out.shape[0] - own
        for k in range(size // LANES):
            block = rows[k * depth : (k + 1) * depth]
            if block.shape[0] < depth:
                block = jnp.concatenate([block, jnp.zeros((depth - block.shape[0], LANES), BF16)], axis=0)
            out[own:, k * LANES : (k + 1) * LANES] = block


def add_kernel(*refs):
    chunks, (sum_ref, first_ref, second_ref) = refs[:4], refs[4:]
    own = sum_ref.shape[0]
    sum_ref[...] = summed([ref[:own, :].astype(F32) for ref in chunks]).astype(BF16)
    for chunk, edge in ((chunks[1], first_ref), (chunks[3], second_ref)):
        parts = [chunk[own:, k * LANES : (k + 1) * LANES] for k in range(chunk.shape[1] // LANES)]
        rows = jnp.concatenate(parts, axis=0)
        edge[...] = rows[: edge.shape[0] * edge.shape[1]].reshape(edge.shape)


def place_kernel(*refs):
    place = lax.axis_index("bins")
    size = refs[0].shape[1]
    for mask, ref in enumerate(refs[:-1]):
        columns = pl.ds(pl.multiple_of((place ^ mask) * size, LANES), size)
        refs[-1][:, columns] = ref[...]


def halves_kernel(one_ref, two_ref, first_ref, second_ref):
    middle = first_ref.shape[1]
    first_ref[...] = one_ref[:, :middle]
    second_ref[...] = two_ref[:, middle:]


def pack_kernel(*refs):
    own, half = refs[0].shape[0], refs[-1].shape[1]
    for j, ref in enumerate(refs[:-1]):
        refs[-1][j * own : (j + 1) * own, :] = ref[:, :half]


def both_kernel(mixed_ref, grad_ref, both_ref):
    rows = mixed_ref.shape[0]
    own = LANES // 4 * 3
    lane = lax.broadcasted_iota(jnp.int32, (rows, LANES), 1)
    moved = pltpu.roll(mixed_ref[...].astype(F32), own, 1)
    both_ref[:rows, :] = jnp.where(lane < own, grad_ref[...].astype(F32), moved).astype(BF16)
    both_ref[rows:, :] = jnp.where(
        lane[: rows // 2] < LANES // 2, moved[: rows // 2], pltpu.roll(moved[rows // 2 :], LANES // 2, 1)
    ).astype(BF16)


def edges_kernel(count, first_ref, second_ref, edges_ref):
    first, last = inner(count)
    for i in range(first_ref.shape[0]):
        before, after = edges_of(first_ref, second_ref, i)
        start = 2 * i * HALO
        edges_ref[start : start + HALO, :] = (before * first).astype(BF16)
        edges_ref[start + HALO : start + 2 * HALO, :] = (after * last).astype(BF16)


def fill_kernel(*refs):
    halves, (first_other, rest_other, weight_ref) = refs[:4], refs[4:]
    own = first_other.shape[0]
    count = len(halves)
    others = [first_other] + [rest_other.at[j * own : (j + 1) * own] for j in range(count - 1)]
    taps, _, width = weight_ref.shape
    step = taps // 2

    def put(low_refs, high_refs):
        for k in range(taps):
            column = k % step * width
            for j, ref in enumerate(low_refs if k < step else high_refs):
                weight_ref[k, j * LANES : j * LANES + own, :] = ref[:, column : column + width]
                weight_ref[k, j * LANES + own : (j + 1) * LANES, :] = jnp.zeros(
                    (LANES - own, width), BF16
                )

    side = lax.axis_index("seqs")

    @pl.when(side == 0)
    def _():
        put(halves, others)

    @pl.when(side != 0)
    def _():
        put(others, halves)


def branch_kernel(x_ref, weight_ref, *refs):
    blocks, output_ref = refs[:4], refs[4]
    seqs, bins, width = x_ref.shape
    rows = seqs * bins
    rest = LANES // 4
    lane = lax.broadcasted_iota(jnp.int32, (bins, LANES), 1)
    for i in range(seqs):
        mixed = []
        for block in blocks:
            start = rows + i * bins % (rows // 2)
            shift = rest + (LANES // 2 if i >= seqs // 2 else 0)
            mixed.append(
                jnp.where(
                    lane < rest,
                    pltpu.roll(block[i * bins : (i + 1) * bins, :].astype(F32), rest, 1),
                    pltpu.roll(block[start : start + bins, :].astype(F32), shift, 1),
                ).astype(BF16)
            )
        branch = dot(jnp.concatenate(mixed, axis=1), weight_ref[weight_ref.shape[0] - 1])
        output_ref[i] = (x_ref[i].astype(F32) + branch).astype(BF16)


def tail_kernel(x_ref, upstream_ref, stat_ref, weight_ref, *refs):
    blocks, edges, (grad_ref, sums_ref, wide_ref) = refs[:4], refs[4:8], refs[8:]
    seqs, bins, width = x_ref.shape
    taps = weight_ref.shape[0] - 1
    mean, rstd = stat_ref[0:1, :], stat_ref[1:2, :]
    gain, bias = stat_ref[3:4, :], stat_ref[4:5, :]
    first = second = 0.0
    for i in range(seqs):
        for j, block in enumerate(blocks):
            lanes = slice(j * LANES, (j + 1) * LANES)
            outer, start = edges[j], 2 * i * HALO
            wide_ref[:HALO, lanes] = outer[start : start + HALO, :].astype(F32)
            wide_ref[HALO : HALO + bins, lanes] = block[i * bins : (i + 1) * bins, :].astype(F32)
            wide_ref[HALO + bins :, lanes] = outer[start + HALO : start + 2 * HALO, :].astype(F32)
        x = x_ref[i].astype(F32)
        act = 0.0
        for k in range(taps):
            start = HALO - (k - taps // 2) * DILATION_STEP
            act += dot(wide_ref[start : start + bins, :].astype(BF16), weight_ref[k])
        value = x * gain + bias
        sigma = sigmoid(value)
        grad = act * (sigma + 1.702 * value * sigma * (1.0 - sigma))
        grad_ref[i] = upstream_ref[i].astype(F32) + gain * grad
        norm = (x - mean) * rstd
        first += jnp.sum(grad * norm, axis=0, keepdims=True)
        second += jnp.sum(grad, axis=0, keepdims=True)
    sums_ref[...] = rows_of(first, second)


def input_grad_kernel(start, total_ref, grad_ref, x_ref, stat_ref, valid_ref, *refs):
    out_ref, left = refs[-2:]
    width = x_ref.shape[2]
    sums = total_ref[...]
    mean, rstd, counted, gain = (stat_ref[k : k + 1, :] for k in range(4))
    slope = gain / counted * rstd * sums[0:1]
    level = gain / counted * sums[1:2] - mean * slope
    copies = []
    if start == 0:
        params_ref, momentum_ref, out_any, moment_any, new_any, moment_ref, new_ref, sems = refs[:8]
        moment = MOMENT_NORM * momentum_ref[...] + sums[:2]
        moment_ref[...] = moment
        new_ref[...] = params_ref[...] - RATE_NORM * moment
        copies = [
            pltpu.make_async_copy(moment_ref, moment_any, sems.at[0]),
            pltpu.make_async_copy(new_ref, new_any, sems.at[1]),
        ]
        for copy in copies:
            copy.start()
    else:
        out_any = refs[1]
    for i in range(out_ref.shape[0]):
        mask = jnp.concatenate([mask_of(valid_ref, start + i)] * (width // LANES), axis=1)
        out_ref[i] = grad_ref[start + i] - mask * (level + x_ref[start + i].astype(F32) * slope)
        copies.append(pltpu.make_async_copy(out_ref.at[i], out_any.at[start + i], left.at[i]))
        copies[-1].start()
    for copy in copies:
        copy.wait()


def split2(value):
    high = value.astype(BF16)
    return high, (value - high.astype(F32)).astype(BF16)


def split3(value):
    high, mid = split2(value)
    rest = value - high.astype(F32) - mid.astype(F32)
    return high, mid, rest.astype(BF16)


def triple(l1, l2, r1, r2):
    return dot(
        jnp.concatenate([l1, l1, l2], axis=1), jnp.concatenate([r1, r2, r1], axis=0)
    )


def product_fine(left, right):
    l1, l2, l3 = split3(left)
    r1, r2, r3 = split3(right)
    return dot(
        jnp.concatenate([l1, l1, l2, l2, l1, l3], axis=1),
        jnp.concatenate([r1, r2, r1, r2, r3, r1], axis=0),
    )


def gram_kernel(right, *refs):
    parameters, parts = refs[:5], refs[5:9]
    high_ref, low_ref, gram_ref = refs[9:]
    size, width = parts[0].shape
    half = width // 2
    base = half if right else 0
    for j, part in enumerate(parts):
        if j < 3:
            source = parameters[j][:, width:]
        else:
            source = jnp.concatenate([parameters[3][:, width:], parameters[4][...]], axis=1)
        momentum = (
            source[:, base : base + half].astype(F32)
            + source[:, width + base : width + base + half].astype(F32)
        )
        high, low = split2(MOMENT_CONV * momentum + part[:, base : base + half].astype(F32))
        high_ref[j * size : (j + 1) * size, :] = high
        low_ref[j * size : (j + 1) * size, :] = low
    high = high_ref[...]
    cross = dot_rows(high, low_ref[...])
    gram_ref[...] = dot_rows(high, high) + (cross + cross.T)


def newton_kernel(own, left_ref, right_ref, other_ref, factor_ref):
    first = (lax.axis_index("seqs") == 0).astype(F32)
    gram = right_ref[...] + first * (left_ref[...] + other_ref[...])
    size = gram.shape[0]
    diagonal = lax.broadcasted_iota(jnp.int32, (size, size), 0) == lax.broadcasted_iota(
        jnp.int32, (size, size), 1
    )
    scale = jnp.sqrt(jnp.sum(jnp.where(diagonal, gram, 0.0), keepdims=True)) + GUARD_EPSILON
    gram = gram / (scale * scale)
    ones = jnp.where(diagonal, NEWTON_A, 0.0)
    factor = None
    for sweep in range(NS_ITERS):
        if sweep == 0:
            g1, g2 = split2(gram)
            poly = ones + NEWTON_B * gram + NEWTON_C * triple(g1, g2, g1, g2)
            factor = poly[:own, :] / scale
            g1, g2 = split2(product_fine(gram, poly))
            gram = triple(g1, g2, *split2(poly))
            continue
        g1, g2 = split2(gram)
        f1, f2 = split2(factor)
        if sweep == NS_ITERS - 1:
            once = triple(f1, f2, g1, g2)
            factor = NEWTON_A * factor + NEWTON_B * once + NEWTON_C * triple(*split2(once), g1, g2)
            continue
        poly = ones + NEWTON_B * gram + NEWTON_C * triple(g1, g2, g1, g2)
        p1, p2 = split2(poly)
        both = triple(
            jnp.concatenate([g1, f1], axis=0), jnp.concatenate([g2, f2], axis=0), p1, p2
        )
        factor = both[size:, :]
        g1, g2 = split2(both[:size, :])
        gram = triple(g1, g2, p1, p2)
    factor_ref[...] = factor


def product_of(factor, high, low):
    f1, f2 = split2(factor)
    return (dot(f1, high) + (dot(f2, high) + dot(f1, low))).astype(BF16)


def right_kernel(own_ref, high_ref, low_ref, step_ref):
    step_ref[...] = product_of(own_ref[...], high_ref[...], low_ref[...])


def left_kernel(own_ref, other_ref, high_ref, low_ref, step_ref):
    factor = jnp.where(lax.axis_index("seqs") == 0, own_ref[...], other_ref[...])
    step_ref[...] = product_of(factor, high_ref[...], low_ref[...])


def halves_of(half_ref, other_ref, use):
    side = lax.axis_index("seqs")

    @pl.when(side == 0)
    def _():
        use(half_ref, other_ref)

    @pl.when(side != 0)
    def _():
        use(other_ref, half_ref)


def moment_kernel(half_ref, other_ref, one_ref, two_ref, moment_one, moment_two):
    half = half_ref.shape[1]
    split = one_ref.shape[1] - half

    def use(low_ref, high_ref):
        moment_one[:, :half] = MOMENT_CONV * one_ref[:, :half] + low_ref[...].astype(F32)
        moment_one[:, half:] = MOMENT_CONV * one_ref[:, half:] + high_ref[:, :split].astype(F32)
        moment_two[...] = MOMENT_CONV * two_ref[...] + high_ref[:, split:].astype(F32)

    halves_of(half_ref, other_ref, use)


def finish_kernel(rate_one, rate_two, left_ref, right_ref, left_other, right_other, one_ref, two_ref, *refs):
    outs, held, sems = refs[:4], refs[4:8], refs[8]
    new_one, low_one, new_two, low_two = held
    width = two_ref.shape[1]
    side = lax.axis_index("seqs")

    def sent(k, slot, columns):
        copy = pltpu.make_async_copy(held[k].at[:, columns], outs[k].at[:, columns], sems.at[slot])
        copy.start()
        return copy

    def use(blocks):
        copies = []
        for k, block in enumerate(blocks):
            last = k == len(blocks) - 1
            columns = slice(0, width) if last else slice(k * width, (k + 1) * width)
            new_ref, low_ref = (new_two, low_two) if last else (new_one, low_one)
            old = two_ref[...] if last else one_ref[:, columns]
            value = old - (rate_two if last else rate_one) * block[...].astype(F32)
            new_ref[:, columns] = value
            low_ref[:, columns] = value.astype(BF16)
            copies += [sent(2 * last, 2 * k, columns), sent(2 * last + 1, 2 * k + 1, columns)]
        for copy in copies:
            copy.wait()

    @pl.when(side == 0)
    def _():
        use([left_ref, right_ref, left_other, right_other])

    @pl.when(side != 0)
    def _():
        use([left_other, right_other, left_ref, right_ref])


def call(kernel, outs, args, name, flops, mebibytes, scratch=(), outside=(), outside_outs=(), aliases=None):
    specs = [
        pl.BlockSpec(memory_space=pltpu.HBM if i in outside else pltpu.VMEM) for i in range(len(args))
    ]
    operands = [
        pltpu.with_memory_space_constraint(v, pltpu.HBM) if i in outside else v
        for i, v in enumerate(args)
    ]
    outs = [jax.ShapeDtypeStruct(shape, dtype) for shape, dtype in outs]
    nbytes = sum(math.prod(v.shape) * v.dtype.itemsize for v in list(args) + outs)
    return pl.pallas_call(
        kernel,
        out_shape=tuple(outs),
        in_specs=specs,
        out_specs=tuple(
            pl.BlockSpec(memory_space=pltpu.HBM if i in outside_outs else pltpu.VMEM)
            for i in range(len(outs))
        ),
        scratch_shapes=list(scratch),
        input_output_aliases=aliases or {},
        compiler_params=pltpu.CompilerParams(vmem_limit_bytes=mebibytes * 2**20),
        cost_estimate=pl.CostEstimate(flops=flops, bytes_accessed=nbytes, transcendentals=0),
        name=name,
    )(*operands)


def shards(
    inputs,
    valid_bins,
    cotangent,
    conv1_weight,
    conv1_momentum,
    conv2_weight,
    conv2_momentum,
    norm1_params,
    norm1_momentum,
    norm2_params,
    norm2_momentum,
):
    seqs, bins, chan = inputs.shape
    rows = seqs * bins
    padded = bins + 2 * HALO
    own = conv1_weight.shape[1]
    taps = conv1_weight.shape[0] // chan
    conv1_rows = taps * chan
    all_rows = conv1_rows + chan
    half = all_rows // 2
    split = conv1_rows - half
    bins_count = lax.axis_size("bins")
    hid = own * lax.axis_size("chan")
    weight_t, momentum_t = conv1_weight.T, conv1_momentum.T

    sums, head, tail = call(
        stats_kernel,
        [((8, chan), F32), ((seqs, HALO, chan), BF16), ((seqs, HALO, chan), BF16)],
        [inputs, valid_bins], "stats", 5 * rows * chan, 10,
        [pltpu.VMEM(inputs.shape, BF16), pltpu.VMEM((seqs, bins), jnp.int32),
         pltpu.SemaphoreType.DMA((seqs + 1,))], (0, 1),
    )
    first, second = exchanged(head, tail)

    owned = [weight_t, conv2_weight, momentum_t, conv2_momentum]
    parameters, weights_other, low_one, low_two = call(
        prep_kernel,
        [((own, 3 * half), BF16), ((own, half), BF16), ((taps * LANES, chan), BF16), ((LANES, chan), BF16)],
        [sums] + owned, "prep", 6 * own * half, 12,
        [pltpu.VMEM(v.shape, F32) for v in owned] + [pltpu.SemaphoreType.DMA((4,))], (1, 2, 3, 4),
    )
    paired = sums + flipped(sums, "seqs", 1)
    paired, sent = tied(paired, parameters)
    parameters_one, parameters_two = flipped(sent, "chan", 1), flipped(sent, "chan", 2)
    if short("bins"):
        total = paired + flipped(paired, "bins", 1)
        total, first, second = tied(total, first, second)
        total = total + flipped(total, "bins", 2)
    else:
        total = lax.psum(paired, "bins")
    pieces = [total]

    act, hidden, sums, stat_one = call(
        functools.partial(conv_kernel, len(pieces), lax.axis_size("bins")),
        [((seqs, padded, chan), BF16), ((rows, LANES), F32), ((8, LANES), F32), ((8, chan), F32)],
        pieces + [inputs, first, second, norm1_params, low_one, valid_bins],
        "conv", 2 * seqs * padded * chan * taps * LANES, 14,
        [pltpu.VMEM((padded, taps * LANES), F32)],
    )
    upstream = cotangent.reshape(rows, chan)
    (back,) = call(
        back_kernel, [((rows, LANES), F32)], [upstream, low_two], "back", 2 * rows * chan * LANES, 6,
    )

    params_two = jnp.pad(norm2_params, ((0, 0), (0, LANES - own)))
    pieces = terms(sums + flipped(sums, "seqs", 1))
    pieces, parameters_one, parameters_two, back = tied(pieces, parameters_one, parameters_two, back)
    middle = 3 * half // 2
    first, second = call(
        halves_kernel, [((own, middle), BF16), ((own, middle), BF16)], [parameters_one, parameters_two],
        "halves", 1, 6,
    )
    parameters_three = [flipped(first, "chan", 2), flipped(second, "chan", 1)]
    mixed, grad, sums, stat_two = call(
        functools.partial(mix_kernel, len(pieces)),
        [((rows, LANES), BF16), ((rows, LANES), F32), ((8, LANES), F32), ((8, LANES), F32)],
        pieces + [stat_one, params_two, hidden, back], "mix", 30 * rows * LANES, 8,
    )
    total = sums + flipped(sums, "seqs", 1)
    pieces = terms(total)
    keep, give, grad_hidden, first, second = call(
        functools.partial(grads_kernel, len(pieces)),
        [((own, half), F32), ((own, half), BF16), ((rows, LANES), BF16),
         ((seqs, HALO, LANES), BF16), ((seqs, HALO, LANES), BF16)],
        pieces + [stat_two, params_two, hidden, grad, valid_bins, mixed, act, upstream],
        "grads", 2 * seqs * padded * chan * taps * LANES, 16,
        [pltpu.VMEM((seqs * padded, taps * LANES), F32)],
    )

    norm2_moment = MOMENT_NORM * norm2_momentum + summed(pieces)[:2, :own]
    norm2_new = norm2_params - RATE_NORM * norm2_moment

    taken = flipped(give, "seqs", 1)
    taken, parameters_three = tied(taken, parameters_three)
    (both,) = call(
        both_kernel, [((rows + rows // 2, LANES), BF16)], [mixed, grad_hidden], "both", 1, 6
    )
    both_one, both_two = flipped(both, "chan", 1), flipped(both, "chan", 2)
    parameters = [parameters, parameters_one, parameters_two] + parameters_three
    packed_from = parameters[1:4]
    if short("bins"):
        size = half // bins_count
        depth = -(-seqs * HALO * LANES // size // 16) * 16
        chunk, deep = ((own, size), BF16), ((own + depth, size), BF16)
        chunks = call(
            pair_kernel, [chunk, deep, chunk, deep], [keep, taken, first, second], "pair", own * half, 6
        )
        chunks = [
            c if m == 0 else flipped(c, "bins", m) for m, c in reversed(list(enumerate(chunks)))
        ][::-1]
        chunks, both_one, both_two = tied(chunks, both_one, both_two)
        edge = ((seqs, HALO, LANES), BF16)
        sum_half, first, second = call(add_kernel, [chunk, edge, edge], chunks, "add", own * half, 6)
        sum_half, sent, packed_from = tied(sum_half, both, packed_from)
    else:
        sum_half = keep + taken.astype(F32)
        first, second = exchanged(first, second)
        sent = both
    border = 2 * seqs * HALO
    (edges,) = call(
        functools.partial(edges_kernel, bins_count), [((border, LANES), BF16)], [first, second], "edges", 1, 4
    )
    both_three = flipped(sent, "chan", 3)
    (packed,) = call(pack_kernel, [((3 * own, half), BF16)], packed_from, "pack", 1, 8)
    weights_rest = flipped(packed, "seqs", 1)
    (filled,) = call(
        fill_kernel, [((taps + 1, 4 * LANES, chan), BF16)],
        parameters[:4] + [weights_other, weights_rest], "fill", 1, 12,
    )
    filled, edges = tied(filled, edges)
    edges = partners(edges, "chan")
    both = [both, both_one, both_two, both_three]
    if short("bins"):
        totals = partners(sum_half, "bins")
        totals, filled = tied(totals, filled)
        (grads_half,) = call(
            place_kernel, [((own, half), BF16)], totals, "place", own * half, 4,
        )
    else:
        grads_half = lax.psum(sum_half, "bins").astype(BF16)
    gathered = partners(grads_half, "chan")

    grad_one, sums = call(
        tail_kernel,
        [((seqs, bins, chan), F32), ((8, chan), F32)],
        [inputs, cotangent, stat_one, filled] + both + edges,
        "tail", 2 * rows * chan * taps * 4 * LANES, 18, [pltpu.VMEM((padded, 4 * LANES), F32)],
    )
    (output,) = call(
        branch_kernel, [((seqs, bins, chan), BF16)], [inputs, filled] + both, "branch",
        2 * rows * chan * 4 * LANES, 14,
    )
    sums_one = sums + flipped(sums, "seqs", 1)
    if short("bins"):
        sums_one = sums_one + flipped(sums_one, "bins", 1)
    grads_half, sums = tied(grads_half, sums)
    grads_other = flipped(grads_half, "seqs", 1)
    conv1_moment, conv2_moment = call(
        moment_kernel, [((own, conv1_rows), F32), ((own, chan), F32)],
        [grads_half, grads_other, momentum_t, conv2_momentum], "moment", 2 * own * all_rows, 12,
    )
    (
        gathered, output, grad_one, sums_one, norm2_moment, norm2_new, conv1_moment, conv2_moment
    ) = tied(
        gathered, output, grad_one, sums_one, norm2_moment, norm2_new, conv1_moment, conv2_moment
    )

    square, wide = ((hid, hid), F32), ((hid, half // 2), BF16)
    (high_left, low_left, gram_left), (high_right, low_right, gram_right) = [
        call(
            functools.partial(gram_kernel, right), [wide, wide, square], parameters + gathered,
            "gram_right" if right else "gram_left", 4 * hid * hid * half, 12,
        )
        for right in (False, True)
    ]
    gram_other = flipped(gram_left, "seqs", 1)
    (own_factor,) = call(
        functools.partial(newton_kernel, own), [((own, hid), F32)],
        [gram_left, gram_right, gram_other], "newton", 100 * hid**3, 14,
    )
    if short("bins"):
        last = flipped(sums_one, "bins", 2)
        own_factor, last = tied(own_factor, last)
        sums_one = sums_one + last
    else:
        sums_one = lax.psum(sums_one, "bins")
    other_factor = flipped(own_factor, "seqs", 1)
    quarter = ((own, half // 2), BF16)
    (right,) = call(right_kernel, [quarter], [own_factor, high_right, low_right], "right", 3 * own * hid * half, 8)
    field = [grad_one, inputs, stat_one, valid_bins]
    middle = seqs // 2
    buffer = [pltpu.VMEM((middle, bins, chan), F32), pltpu.SemaphoreType.DMA((middle,))]
    input_grad, norm1_moment, norm1_new = call(
        functools.partial(input_grad_kernel, 0),
        [((seqs, bins, chan), F32), ((2, chan), F32), ((2, chan), F32)],
        [sums_one] + field + [norm1_params, norm1_momentum], "input_grad", 5 * rows * chan, 16,
        [pltpu.VMEM((2, chan), F32), pltpu.VMEM((2, chan), F32), pltpu.SemaphoreType.DMA((2,))] + buffer,
        (), (0, 1, 2),
    )
    other_factor, input_grad = tied(other_factor, input_grad)
    (left,) = call(
        left_kernel, [quarter], [own_factor, other_factor, high_left, low_left], "left", 3 * own * hid * half, 8
    )
    step_other = [flipped(left, "seqs", 1), flipped(right, "seqs", 1)]
    (input_grad,) = call(
        functools.partial(input_grad_kernel, middle), [((seqs, bins, chan), F32)],
        [sums_one] + field + [input_grad], "input_grad_rest", 5 * rows * chan, 16,
        buffer, (5,), (0,), {5: 0},
    )
    conv1_new, conv1_low, conv2_new, conv2_low = call(
        functools.partial(
            finish_kernel,
            RATE_CONV * math.sqrt(max(1.0, conv1_rows / hid)),
            RATE_CONV * math.sqrt(max(1.0, chan / hid)),
        ),
        [((own, conv1_rows), F32), ((own, conv1_rows), BF16), ((own, chan), F32), ((own, chan), BF16)],
        [left, right] + step_other + [weight_t, conv2_weight], "finish", 2 * own * all_rows, 12,
        [pltpu.VMEM((own, conv1_rows), F32), pltpu.VMEM((own, conv1_rows), BF16),
         pltpu.VMEM((own, chan), F32), pltpu.VMEM((own, chan), BF16), pltpu.SemaphoreType.DMA((8,))],
        (), (0, 1, 2, 3),
    )
    return (
        output,
        input_grad,
        conv1_moment.T,
        conv1_new.T,
        conv1_low.T,
        conv2_moment,
        conv2_new,
        conv2_low,
        norm1_moment,
        norm1_new,
        norm2_moment,
        norm2_new,
    )


def solution(mesh):
    placed = (
        P("seqs", "bins", None),
        P("seqs", "bins"),
        P("seqs", "bins", None),
        P(None, "chan"),
        P(None, "chan"),
        P("chan", None),
        P("chan", None),
        P(),
        P(),
        P(None, "chan"),
        P(None, "chan"),
    )
    return jax.shard_map(
        shards,
        mesh=mesh,
        in_specs=placed,
        out_specs=(
            P("seqs", "bins", None),
            P("seqs", "bins", None),
            P(None, "chan"),
            P(None, "chan"),
            P(None, "chan"),
            P("chan", None),
            P("chan", None),
            P("chan", None),
            P(),
            P(),
            P(None, "chan"),
            P(None, "chan"),
        ),
        check_vma=False,
    )
```
